32 devices in a mesh: groups: 2 (over y), lat: 4 (over z), lon: 2 (over x), ens: 2 (over core).
Axes of the slice: x: 2, y: 2, z: 4, core: 2. Of those that a mesh axis runs over, the one named last changes fastest.
Arguments:
- fields: bfloat16 [4, 8, 1440, 384], P(('groups', 'ens'), 'lat', 'lon'), parts along dimension 0, may hold values from -6 to 6
- cotangent: bfloat16 [4, 8, 1440, 384], P(('groups', 'ens'), 'lat', 'lon'), parts along dimension 0, may hold values from -6 to 6
- filter_one: bfloat16 [8, 3, 9, 9], replicated, may hold values from -1.25 to 1.25
- filter_two: bfloat16 [8, 3, 9, 9], replicated, may hold values from -1.25 to 1.25
- mix_one: bfloat16 [432, 384], replicated, may hold values from -0.3125 to 0.3125
- mix_two: bfloat16 [432, 384], replicated, may hold values from -0.3125 to 0.3125
- source_rows: int32 [8, 3], replicated, may hold values from 0 to 7, as said below
- band_width: int32 [8, 3], replicated, may hold values from 1 to 4, as said below
Outputs:
- forward: bfloat16 [4, 8, 1440, 384], P(('groups', 'ens'), 'lat', 'lon'), parts along dimension 0
- adjoint: bfloat16 [4, 8, 1440, 384], P(('groups', 'ens'), 'lat', 'lon'), parts along dimension 0
- grad_one: float32 [864, 384], P('groups'), parts along dimension 0
- grad_two: float32 [864, 384], P('groups'), parts along dimension 0
The draws below stay inside these ranges and needn't reach their ends.
There are 2 independent parts, one for each index of `groups`. The reference program is written for one: setup_inputs(seed, part) draws one part's arguments, and reference() takes and returns one part's arrays. A program takes and returns all parts, laid end to end along the dimension named above; an argument that names none is the same for every part. Nothing has to cross between parts.
Inputs may be any that keep to these rules, and one draw needn't show every extreme that they name: `source_rows`: row i lists i itself, then a row at most 2 below it and a row at most 2 above it, each clipped to the band; the distance 2 occurs. `band_width`: rows within 2 of either end of the band use the full half-width.
All inputs are finite; a program needn't handle non-finite values.
Results may differ from the reference program's by a relative error of at most 0.0067.
Values may be sent and summed in bfloat16 or wider, within the bound.
A program may use at most 192 MiB of HBM per device.

```python
import jax
import jax.numpy as jnp
from jax import lax

C = 384
K = 9
G = 8
NLON = 1440
SRC = 3
HALO_R = 2
WHALF = 4
WIN = 9
CG = 48
NLAT = 8
MEMBERS = 2


def draw_source_rows(key, part):
    key = jax.random.fold_in(key, 11)
    key_below, key_above = jax.random.split(key)
    rows = jnp.arange(NLAT, dtype=jnp.int32)
    below = jax.random.randint(key_below, (NLAT,), 1, HALO_R + 1, dtype=jnp.int32)
    above = jax.random.randint(key_above, (NLAT,), 1, HALO_R + 1, dtype=jnp.int32)
    below = jnp.where(rows % 4 == 0, HALO_R, below)
    above = jnp.where(rows % 4 == 2, HALO_R, above)
    lower = jnp.clip(rows - below, 0, NLAT - 1)
    upper = jnp.clip(rows + above, 0, NLAT - 1)
    return jnp.stack([rows, lower, upper], axis=1).astype(jnp.int32)


def draw_band_width(key, part):
    key = jax.random.fold_in(key, 23)
    rows = jnp.arange(NLAT, dtype=jnp.int32)[:, None]
    slots = jnp.arange(SRC, dtype=jnp.int32)[None, :]
    widths = jax.random.randint(key, (NLAT, SRC), 1, WHALF + 1, dtype=jnp.int32)
    widths = jnp.where((rows % 4 == 1) & (slots == 0), WHALF, widths)
    widths = jnp.where((rows % 4 == 3) & (slots == SRC - 1), 1, widths)
    polar = (rows < HALO_R) | (rows >= NLAT - HALO_R)
    return jnp.where(polar, WHALF, widths).astype(jnp.int32)


def steps_of(key, extent, cuts, least, high):
    gain = 1.0
    for dim, parts in cuts:
        draws = jax.random.uniform(jax.random.fold_in(jax.random.fold_in(key, 6), dim), (parts,), jnp.float32, least / len(cuts), high / len(cuts))
        gain = gain * jnp.repeat(jnp.exp(draws), extent[dim] // parts).reshape((-1,) + (1,) * (len(extent) - 1 - dim))
    return gain


def centred(key, extent, width, limit, shards=(), held_as=jnp.bfloat16):
    values = width * jax.random.normal(key, extent, jnp.float32)
    if shards:
        values = values * steps_of(key, extent, shards, -0.22, 0.18)
    return jnp.clip(values, -limit, limit).astype(held_as)


def setup_inputs(seed: int = 0, part: int = 0) -> dict:
    splits = jax.random.split(jax.random.key(seed), 9)
    part_splits = jax.random.split(jax.random.fold_in(splits[8], part), 9)
    return {
        "fields": centred(part_splits[0], (MEMBERS, NLAT, NLON, C), 1.0, 6.0, ((0, 2), (1, 4), (2, 2))),
        "cotangent": centred(part_splits[1], (MEMBERS, NLAT, NLON, C), 1.0, 6.0, ((0, 2), (1, 4), (2, 2))),
        "filter_one": centred(splits[2], (NLAT, SRC, K, WIN), (SRC * WIN) ** -0.5, 1.25),
        "filter_two": centred(splits[3], (NLAT, SRC, K, WIN), (SRC * WIN) ** -0.5, 1.25),
        "mix_one": centred(splits[4], (K * CG, C), (K * CG) ** -0.5, 0.3125),
        "mix_two": centred(splits[5], (K * CG, C), (K * CG) ** -0.5, 0.3125),
        "source_rows": draw_source_rows(jax.random.fold_in(splits[8], 71), part),
        "band_width": draw_band_width(jax.random.fold_in(splits[8], 71), part),
    }


def masked_filters(filt, band_width):
    offsets = jnp.abs(jnp.arange(WIN, dtype=jnp.int32) - WHALF)
    keep = offsets[None, None, :] <= band_width[:, :, None]
    return filt * keep[:, :, None, :].astype(filt.dtype)

def basis_apply(kernel, source_slab):
    return lax.conv_general_dilated(source_slab.astype(jnp.float32), jnp.transpose(kernel.astype(jnp.float32), (1, 0, 2)), (1,), 'VALID', dimension_numbers=('CHN', 'OIH', 'CHN'), preferred_element_type=jnp.float32)

def basis_adjoint(kernel, grad_row):
    margin = kernel.shape[2] - 1
    return lax.conv_general_dilated(grad_row.astype(jnp.float32), jnp.flip(kernel.astype(jnp.float32), 2), (1,), ((margin, margin),), dimension_numbers=('CHN', 'OIH', 'CHN'), preferred_element_type=jnp.float32)

def split_weights(weights):
    return weights.astype(jnp.float32).reshape(K, CG, G, CG)

def mix_row(coeffs, weights):
    split = coeffs.astype(jnp.float32).reshape(K, coeffs.shape[1], G, CG)
    out = jnp.einsum('kjgc,kcgo->jgo', split, split_weights(weights))
    return out.reshape(coeffs.shape[1], C)

def mix_row_adjoint(grad_row, weights):
    split = grad_row.astype(jnp.float32).reshape(grad_row.shape[0], G, CG)
    out = jnp.einsum('jgo,kcgo->kjgc', split, split_weights(weights))
    return out.reshape(K, grad_row.shape[0], C)

def weight_row(coeffs, grad_row):
    left = coeffs.astype(jnp.float32).reshape(K, coeffs.shape[1], G, CG)
    right = grad_row.astype(jnp.float32).reshape(grad_row.shape[0], G, CG)
    return jnp.einsum('kjgc,jgo->kcgo', left, right).reshape(K * CG, C)

def wrap_cols(activ):
    return jnp.concatenate([activ[:, NLON - WHALF:], activ, activ[:, :WHALF]], axis=1)

def layer_forward(activ, kernels, source_rows, weights):
    wrapped = wrap_cols(activ)

    def one_row(item):
        kernel, sources = item
        slab = jnp.take(wrapped, sources, axis=0)
        coeffs = basis_apply(kernel, slab).astype(jnp.bfloat16)
        return (coeffs, mix_row(coeffs, weights))
    return lax.map(one_row, (kernels, source_rows))

def layer_adjoint(grad, coeffs_all, kernels, source_rows, weights):
    spread_init = jnp.zeros((NLAT, NLON + 2 * WHALF, C), jnp.float32)
    weight_init = jnp.zeros((K * CG, C), jnp.float32)

    def add_row(carry, item):
        spread, weight_sum = carry
        kernel, sources, grad_row, coeffs = item
        coeffs_grad = mix_row_adjoint(grad_row, weights).astype(jnp.bfloat16)
        pieces = basis_adjoint(kernel, coeffs_grad)
        spread = spread.at[sources].add(pieces)
        weight_sum = weight_sum + weight_row(coeffs, grad_row)
        return ((spread, weight_sum), None)
    (spread, weight_sum), _ = lax.scan(add_row, (spread_init, weight_init), (kernels, source_rows, grad, coeffs_all))
    middle = spread[:, WHALF:WHALF + NLON]
    middle = middle.at[:, :WHALF].add(spread[:, NLON + WHALF:])
    middle = middle.at[:, NLON - WHALF:].add(spread[:, :WHALF])
    return (middle, weight_sum)

def reference(fields, cotangent, filter_one, filter_two, mix_one, mix_two, source_rows, band_width):
    kernel_one = masked_filters(filter_one, band_width)
    kernel_two = masked_filters(filter_two, band_width)
    forward_list = []
    adjoint_list = []
    grad_one = jnp.zeros((K * CG, C), jnp.float32)
    grad_two = jnp.zeros((K * CG, C), jnp.float32)
    for member in range(MEMBERS):
        coeffs_one, pre_one = layer_forward(fields[member], kernel_one, source_rows, mix_one)
        gate = jax.nn.sigmoid(pre_one)
        hidden = (pre_one * gate).astype(jnp.bfloat16)
        coeffs_two, pre_two = layer_forward(hidden, kernel_two, source_rows, mix_two)
        forward_list.append(pre_two.astype(jnp.bfloat16))
        hidden_grad, part_two = layer_adjoint(cotangent[member], coeffs_two, kernel_two, source_rows, mix_two)
        pre_grad = (hidden_grad * gate * (1.0 + pre_one * (1.0 - gate))).astype(jnp.bfloat16)
        input_grad, part_one = layer_adjoint(pre_grad, coeffs_one, kernel_one, source_rows, mix_one)
        adjoint_list.append(input_grad.astype(jnp.bfloat16))
        grad_one = grad_one + part_one
        grad_two = grad_two + part_two
    factor = 1.0 / jnp.sqrt(jnp.float32(NLAT * NLON * MEMBERS))
    return (jnp.stack(forward_list), jnp.stack(adjoint_list), grad_one * factor, grad_two * factor)
```

```python
import functools

import jax
import jax.numpy as jnp
from jax import lax
from jax.experimental import pallas as pl
from jax.experimental.pallas import tpu as pltpu
from jax.sharding import PartitionSpec as P

K = 9
G = 8
HALO_R = 2
WHALF = 4
WIN = 9
ROWS = 2
NEAR = 2 * HALO_R + 1
TILE = 32
SPAN = TILE + 16
HALF = 256
MARGIN = 16

F32 = jnp.float32
BF16 = jnp.bfloat16


def layer_kernel(mode, width, cols, with_mix, with_grad, *refs):
    refs = list(refs)
    up, own, down, band = refs[:4]
    refs = refs[4:]
    if with_mix:
        weights = refs[:2]
        refs = refs[2:]
    if mode == "scale":
        slope_in = refs.pop(0)
    if with_grad:
        grad_t = refs.pop(0)
    lows, highs = refs[-2:]
    refs = refs[:-2]
    rows = [up.at[0], up.at[1], own.at[0], own.at[1], down.at[0], down.at[1]]

    def basis(b, carry):
        start = pl.multiple_of(b * TILE, TILE)
        for r in range(ROWS):
            slab = jnp.concatenate(
                [rows[r + e][pl.ds(start, SPAN), :] for e in range(NEAR)], axis=0
            )
            out = jnp.dot(band[r], slab, preferred_element_type=F32).astype(BF16)
            at = pl.multiple_of(r * width + start, TILE)
            for k in range(K):
                piece = out[k * TILE : (k + 1) * TILE]
                lows[pl.ds(at, TILE), k * HALF : (k + 1) * HALF] = piece[:, :HALF]
                highs[pl.ds(at, TILE), k * HALF : (k + 1) * HALF] = piece[:, 128:]
        return carry

    lax.fori_loop(0, width // TILE, basis, 0)

    if with_mix:
        step = width // 2

        def mix(r, carry):
            for part in range(2):
                at = pl.multiple_of(r * width + part * step, 16)
                low = jnp.dot(lows[pl.ds(at, step), :], weights[0][...], preferred_element_type=F32)
                high = jnp.dot(highs[pl.ds(at, step), :], weights[1][...], preferred_element_type=F32)
                total = jnp.concatenate(
                    [low[:, :128], low[:, 128:] + high[:, :128], high[:, 128:]], axis=1
                )
                span = slice(part * step, (part + 1) * step)
                if mode == "gate":
                    gate = jax.nn.sigmoid(total)
                    refs[0][r, span, :] = (total * gate).astype(BF16)
                    refs[1][r, span, :] = gate * (1.0 + total * (1.0 - gate))
                elif mode == "scale":
                    refs[0][r, span, :] = (total * slope_in[r, span, :]).astype(BF16)
                else:
                    keep = min(step, cols - part * step)
                    refs[0][r, part * step : part * step + keep, :] = total[:keep].astype(BF16)
            if mode != "plain":
                refs[0][r, width : width + MARGIN, :] = jnp.zeros((MARGIN, total.shape[1]), BF16)
            return carry

        lax.fori_loop(0, ROWS, mix, 0)

    if with_grad:
        out = refs[-1]
        depth = lows.shape[0]
        tail = depth - ROWS * width
        if tail:
            lows[ROWS * width :, :] = jnp.zeros((tail, K * HALF), BF16)
            highs[ROWS * width :, :] = jnp.zeros((tail, K * HALF), BF16)
        cg = out.shape[1] // G

        def grad(k, carry):
            at = pl.multiple_of(k * HALF, HALF)
            low = jnp.dot(grad_t[0:HALF, :], lows[:, pl.ds(at, HALF)], preferred_element_type=F32).T
            high = jnp.dot(grad_t[128:, :], highs[:, pl.ds(at, HALF)], preferred_element_type=F32).T
            lane = lax.broadcasted_iota(jnp.int32, (cg, HALF), 1)
            sums = []
            for block, base, groups in ((low, 0, range(4)), (high, 128, range(4, 8))):
                total = jnp.zeros((cg, HALF), F32)
                for g in groups:
                    first = g * cg - base
                    inside = (lane >= first) & (lane < first + cg)
                    total = total + jnp.where(inside, block[first : first + cg], 0.0)
                sums.append(total)
            low, high = sums
            out[pl.ds(pl.multiple_of(k * cg, 8), cg), :] = jnp.concatenate(
                [low[:, :128], low[:, 128:] + high[:, :128], high[:, 128:]], axis=1
            )
            return carry

        lax.fori_loop(0, K, grad, 0)


def layer(mode, cols, halo, band, weights=None, slope=None, grad_t=None):
    chan = halo[1].shape[2]
    width = halo[1].shape[1] - MARGIN
    with_mix, with_grad = weights is not None, grad_t is not None
    args = list(halo) + [band]
    outs = []
    if with_mix:
        args += list(weights)
        held = width + MARGIN if mode != "plain" else cols
        outs.append(jax.ShapeDtypeStruct((ROWS, held, chan), BF16))
    if mode == "gate":
        outs.append(jax.ShapeDtypeStruct((ROWS, width, chan), F32))
    if mode == "scale":
        args.append(slope)
    depth = ROWS * width
    if with_grad:
        args.append(grad_t)
        depth = grad_t.shape[1]
        outs.append(jax.ShapeDtypeStruct((K * chan // G, chan), F32))
    vmem = pl.BlockSpec(memory_space=pltpu.VMEM)
    flops = 2 * ROWS * width * K * HALF * 2 * HALF * (1 + with_mix + with_grad)
    return pl.pallas_call(
        functools.partial(layer_kernel, mode, width, cols, with_mix, with_grad),
        out_shape=tuple(outs),
        in_specs=[vmem] * len(args),
        out_specs=tuple([vmem] * len(outs)),
        scratch_shapes=[pltpu.VMEM((depth, K * HALF), BF16)] * 2,
        compiler_params=pltpu.CompilerParams(vmem_limit_bytes=48 * 2**20),
        cost_estimate=pl.CostEstimate(flops=flops, bytes_accessed=10 * 2**20, transcendentals=0),
    )(*args)


def exchanged(block):
    count = lax.axis_size("lat")
    up = lax.ppermute(block, "lat", [(i, i + 1) for i in range(count - 1)])
    down = lax.ppermute(block, "lat", [(i + 1, i) for i in range(count - 1)])
    return up, block, down


def masked_filters(filt, band_width):
    offsets = jnp.abs(jnp.arange(WIN, dtype=jnp.int32) - WHALF)
    keep = offsets[None, None, :] <= band_width[:, :, None]
    return filt * keep[:, :, None, :].astype(filt.dtype)


def banded(table):
    chosen = (
        jnp.arange(SPAN)[None, None, :] - jnp.arange(TILE)[None, :, None]
        == jnp.arange(WIN)[:, None, None]
    ).astype(BF16)
    out = jnp.einsum("rekw,wtv->rktev", table, chosen, preferred_element_type=F32)
    return out.astype(BF16).reshape(ROWS, K * TILE, NEAR * SPAN)


def filter_tables(kernel, source_rows, first_row):
    pad = HALO_R
    near = jnp.arange(NEAR)
    kernel = jnp.pad(kernel.astype(F32), ((pad, pad), (0, 0), (0, 0), (0, 0)))
    src = jnp.pad(source_rows, ((pad, pad), (0, 0)), constant_values=-1)
    kernel = lax.dynamic_slice_in_dim(kernel, first_row, ROWS + 2 * pad, 0)
    src = lax.dynamic_slice_in_dim(src, first_row, ROWS + 2 * pad, 0)
    own = first_row + jnp.arange(ROWS)
    hit = src[pad : pad + ROWS, :, None] == own[:, None, None] - pad + near
    pull = jnp.einsum("rse,rskw->rekw", hit.astype(F32), kernel[pad : pad + ROWS], precision="highest")
    stack = jnp.stack([kernel[r : r + NEAR] for r in range(ROWS)])
    hit = jnp.stack([src[r : r + NEAR] == own[r] for r in range(ROWS)])
    push = jnp.sum(jnp.where(hit[:, :, :, None, None], stack, 0.0), axis=2)
    return banded(pull.astype(BF16)), banded(jnp.flip(push, 3).astype(BF16))


def dense_mix(weights):
    chan = weights.shape[1]
    cg = chan // G
    tiled = jnp.broadcast_to(weights.reshape(K, 1, cg, chan), (K, G, cg, chan)).reshape(K, chan, chan)
    group = jnp.arange(chan) // cg
    same = group[:, None] == group[None, :]
    wide = jnp.where(same[None], tiled, 0).astype(BF16)
    turned = jnp.swapaxes(wide, 1, 2)
    first = (jnp.arange(chan) < chan // 2)[None, None, :]

    def windows(block):
        low = jnp.where(first, block, 0)[:, :HALF, :HALF]
        high = jnp.where(first, 0, block)[:, chan - HALF :, chan - HALF :]
        return low.reshape(K * HALF, HALF), high.reshape(K * HALF, HALF)

    return windows(wide), windows(turned)


def turned_grad(grad, width, shift):
    chan = grad.shape[2]
    cols = grad.shape[1]
    grad = jnp.pad(grad, ((0, 0), (shift, width - shift - cols), (0, 0)))
    depth = -(-ROWS * width // 256) * 256
    flat = jnp.pad(grad.reshape(ROWS * width, chan), ((0, depth - ROWS * width), (0, 0)))
    return flat.T


def shards(fields, cotangent, filter_one, filter_two, mix_one, mix_two, source_rows, band_width):
    activ = fields[0]
    cot = cotangent[0]
    cols = activ.shape[1]
    wide = 2 * WHALF
    width = -(-(cols + wide) // TILE) * TILE
    total_rows = ROWS * lax.axis_size("lat")
    total_cols = cols * lax.axis_size("lon")
    first_row = lax.axis_index("lat") * ROWS

    lon = lax.axis_size("lon")
    both = jnp.stack([activ, cot])
    left = lax.ppermute(both[:, :, cols - wide :], "lon", [(i, (i + 1) % lon) for i in range(lon)])
    right = lax.ppermute(both[:, :, :wide], "lon", [((i + 1) % lon, i) for i in range(lon)])

    def widened(index, block):
        tail = jnp.zeros((ROWS, width + MARGIN - cols - 2 * wide, block.shape[2]), BF16)
        return jnp.concatenate([left[index], block, right[index], tail], axis=1)

    fields_halo = exchanged(widened(0, activ))
    cot_wide = widened(1, cot)
    cot_halo = exchanged(cot_wide)

    pull_one, push_one = filter_tables(masked_filters(filter_one, band_width), source_rows, first_row)
    pull_two, push_two = filter_tables(masked_filters(filter_two, band_width), source_rows, first_row)
    mix_one_f, mix_one_t = dense_mix(mix_one)
    mix_two_f, mix_two_t = dense_mix(mix_two)
    cot_t = turned_grad(cot, width, 0)

    hidden, slope = layer("gate", cols, fields_halo, pull_one, mix_one_f)
    hidden_halo = exchanged(hidden)
    (pre_grad,) = layer("scale", cols, cot_halo, push_two, mix_two_t, slope=slope)
    pre_halo = exchanged(pre_grad)
    pre_t = turned_grad(pre_grad[:, WHALF : WHALF + cols], width, WHALF)
    (part_one,) = layer("none", cols, fields_halo, pull_one, grad_t=pre_t)
    forward, part_two = layer("plain", cols, hidden_halo, pull_two, mix_two_f, grad_t=cot_t)
    (adjoint,) = layer("plain", cols, pre_halo, push_one, mix_one_t)

    factor = 1.0 / jnp.sqrt(jnp.float32(total_rows * total_cols * lax.axis_size("ens")))
    total_one = lax.psum(part_one, ("lat", "lon", "ens"))
    total_two = lax.psum(part_two, ("lat", "lon", "ens"))
    return forward[None], adjoint[None], total_one * factor, total_two * factor


def solution(mesh):
    field = P(("groups", "ens"), "lat", "lon", None)
    return jax.shard_map(
        shards,
        mesh=mesh,
        in_specs=(field, field, P(), P(), P(), P(), P(), P()),
        out_specs=(field, field, P("groups", None), P("groups", None)),
        check_vma=False,
    )
```

```python
import functools

import jax
import jax.numpy as jnp
from jax import lax
from jax.experimental import pallas as pl
from jax.experimental.pallas import tpu as pltpu
from jax.sharding import PartitionSpec as P

K = 9
G = 8
HALO_R = 2
WHALF = 4
WIN = 9
ROWS = 2
NEAR = 2 * HALO_R + 1
TILE = 32
SPAN = TILE + 16
HALF = 256
MARGIN = 16

F32 = jnp.float32
BF16 = jnp.bfloat16


def group_windows(block, cg):
    lane = lax.broadcasted_iota(jnp.int32, (cg, block.shape[1]), 1)
    low = [jnp.where((lane >= g * cg) & (lane < (g + 1) * cg), block, 0.0) for g in range(G)]
    wide = jnp.concatenate(low[: G // 2], axis=0)[:, :HALF]
    rest = jnp.concatenate(low[G // 2 :], axis=0)[:, 128:]
    gap = jnp.zeros((HALF - wide.shape[0], HALF), F32)
    return jnp.concatenate([wide, gap], axis=0), jnp.concatenate([gap, rest], axis=0)


def layer_kernel(mode, width, cols, turn, valid, with_mix, with_grad, *refs):
    refs = list(refs)
    up, own, down, band = refs[:4]
    refs = refs[4:]
    if with_mix:
        mix_ref = refs.pop(0)
    if mode == "scale":
        slope_in = refs.pop(0)
    if with_grad:
        grad_in = refs.pop(0)
        turned = refs.pop()
        padded = refs.pop()
    if with_mix:
        weights = refs[-2:]
        refs = refs[:-2]
    lows, highs = refs[-2:]
    refs = refs[:-2]
    rows = [up.at[0], up.at[1], own.at[0], own.at[1], down.at[0], down.at[1]]

    if with_mix:
        cg = mix_ref.shape[1] // G

        def spread(k, carry):
            block = mix_ref[pl.ds(pl.multiple_of(k * cg, 16), cg), :].astype(F32)
            at = pl.ds(pl.multiple_of(k * HALF, HALF), HALF)
            for dest, window in zip(weights, group_windows(block, cg)):
                dest[at, :] = (window.T if turn else window).astype(BF16)
            return carry

        lax.fori_loop(0, K, spread, 0)

    def basis(b, carry):
        start = pl.multiple_of(b * TILE, TILE)
        for r in range(ROWS):
            slab = jnp.concatenate(
                [rows[r + e][pl.ds(start, SPAN), :] for e in range(NEAR)], axis=0
            )
            out = jnp.dot(band[r], slab, preferred_element_type=F32).astype(BF16)
            at = pl.multiple_of(r * width + start, TILE)
            for k in range(K):
                piece = out[k * TILE : (k + 1) * TILE]
                lows[pl.ds(at, TILE), k * HALF : (k + 1) * HALF] = piece[:, :HALF]
                highs[pl.ds(at, TILE), k * HALF : (k + 1) * HALF] = piece[:, 128:]
        return carry

    lax.fori_loop(0, width // TILE, basis, 0)

    if with_mix:
        step = width // 2

        def mix(r, carry):
            for part in range(2):
                at = pl.multiple_of(r * width + part * step, 16)
                low = jnp.dot(lows[pl.ds(at, step), :], weights[0][...], preferred_element_type=F32)
                high = jnp.dot(highs[pl.ds(at, step), :], weights[1][...], preferred_element_type=F32)
                total = jnp.concatenate(
                    [low[:, :128], low[:, 128:] + high[:, :128], high[:, 128:]], axis=1
                )
                span = slice(part * step, (part + 1) * step)
                if mode == "gate":
                    gate = jax.nn.sigmoid(total)
                    refs[0][r, span, :] = (total * gate).astype(BF16)
                    refs[1][r, span, :] = gate * (1.0 + total * (1.0 - gate))
                elif mode == "scale":
                    refs[0][r, span, :] = (total * slope_in[r, span, :]).astype(BF16)
                else:
                    keep = min(step, cols - part * step)
                    refs[0][r, part * step : part * step + keep, :] = total[:keep].astype(BF16)
            if mode != "plain":
                refs[0][r, width : width + MARGIN, :] = jnp.zeros((MARGIN, total.shape[1]), BF16)
            return carry

        lax.fori_loop(0, ROWS, mix, 0)

    if with_grad:
        out = refs[-1]
        cg = out.shape[1] // G
        first, last = valid
        size = grad_in.shape[1]
        for r in range(ROWS):
            padded[...] = jnp.zeros(padded.shape, F32)
            here = min(size, width)
            value = grad_in[r, :here, :].astype(F32)
            place = lax.broadcasted_iota(jnp.int32, value.shape, 0)
            padded[:here, :] = jnp.where((place >= first) & (place < last), value, 0.0)
            turned[r] = padded[...].T.astype(BF16)

        def grad(k, carry):
            at = pl.multiple_of(k * HALF, HALF)
            low = jnp.zeros((HALF, HALF), F32)
            high = jnp.zeros((HALF, HALF), F32)
            for r in range(ROWS):
                span = slice(r * width, (r + 1) * width)
                low += jnp.dot(turned[r, 0:HALF, :width], lows[span, pl.ds(at, HALF)], preferred_element_type=F32)
                high += jnp.dot(turned[r, 128:, :width], highs[span, pl.ds(at, HALF)], preferred_element_type=F32)
            low, high = low.T, high.T
            lane = lax.broadcasted_iota(jnp.int32, (cg, HALF), 1)
            sums = []
            for block, base, groups in ((low, 0, range(4)), (high, 128, range(4, 8))):
                total = jnp.zeros((cg, HALF), F32)
                for g in groups:
                    first = g * cg - base
                    inside = (lane >= first) & (lane < first + cg)
                    total = total + jnp.where(inside, block[first : first + cg], 0.0)
                sums.append(total)
            low, high = sums
            out[pl.ds(pl.multiple_of(k * cg, 8), cg), :] = jnp.concatenate(
                [low[:, :128], low[:, 128:] + high[:, :128], high[:, 128:]], axis=1
            )
            return carry

        lax.fori_loop(0, K, grad, 0)


def layer(mode, cols, halo, band, weights=None, turn=False, slope=None, grad=None, valid=None):
    chan = halo[1].shape[2]
    width = halo[1].shape[1] - MARGIN
    with_mix, with_grad = weights is not None, grad is not None
    args = list(halo) + [band]
    outs = []
    if with_mix:
        args.append(weights)
        held = width + MARGIN if mode != "plain" else cols
        outs.append(jax.ShapeDtypeStruct((ROWS, held, chan), BF16))
    if mode == "gate":
        outs.append(jax.ShapeDtypeStruct((ROWS, width, chan), F32))
    if mode == "scale":
        args.append(slope)
    depth = ROWS * width
    if with_grad:
        args.append(grad)
        outs.append(jax.ShapeDtypeStruct((K * chan // G, chan), F32))
    scratch = [pltpu.VMEM((depth, K * HALF), BF16)] * 2
    if with_mix:
        scratch += [pltpu.VMEM((K * HALF, HALF), BF16)] * 2
    if with_grad:
        long = -(-width // 128) * 128
        scratch += [pltpu.VMEM((long, chan), F32), pltpu.VMEM((ROWS, chan, long), BF16)]
    vmem = pl.BlockSpec(memory_space=pltpu.VMEM)
    flops = 2 * ROWS * width * K * HALF * 2 * HALF * (1 + with_mix + with_grad)
    return pl.pallas_call(
        functools.partial(layer_kernel, mode, width, cols, turn, valid, with_mix, with_grad),
        out_shape=tuple(outs),
        in_specs=[vmem] * len(args),
        out_specs=tuple([vmem] * len(outs)),
        scratch_shapes=scratch,
        compiler_params=pltpu.CompilerParams(vmem_limit_bytes=48 * 2**20),
        cost_estimate=pl.CostEstimate(flops=flops, bytes_accessed=10 * 2**20, transcendentals=0),
    )(*args)


def exchanged(block):
    count = lax.axis_size("lat")
    up = lax.ppermute(block, "lat", [(i, i + 1) for i in range(count - 1)])
    down = lax.ppermute(block, "lat", [(i + 1, i) for i in range(count - 1)])
    return up, block, down


def masked_filters(filt, band_width):
    offsets = jnp.abs(jnp.arange(WIN, dtype=jnp.int32) - WHALF)
    keep = offsets[None, None, :] <= band_width[:, :, None]
    return filt * keep[:, :, None, :].astype(filt.dtype)


def banded(table):
    chosen = (
        jnp.arange(SPAN)[None, None, :] - jnp.arange(TILE)[None, :, None]
        == jnp.arange(WIN)[:, None, None]
    ).astype(BF16)
    out = jnp.einsum("rekw,wtv->rktev", table, chosen, preferred_element_type=F32)
    return out.astype(BF16).reshape(ROWS, K * TILE, NEAR * SPAN)


def filter_tables(kernel, source_rows, first_row):
    pad = HALO_R
    near = jnp.arange(NEAR)
    kernel = jnp.pad(kernel.astype(F32), ((pad, pad), (0, 0), (0, 0), (0, 0)))
    src = jnp.pad(source_rows, ((pad, pad), (0, 0)), constant_values=-1)
    kernel = lax.dynamic_slice_in_dim(kernel, first_row, ROWS + 2 * pad, 0)
    src = lax.dynamic_slice_in_dim(src, first_row, ROWS + 2 * pad, 0)
    own = first_row + jnp.arange(ROWS)
    hit = src[pad : pad + ROWS, :, None] == own[:, None, None] - pad + near
    pull = jnp.einsum("rse,rskw->rekw", hit.astype(F32), kernel[pad : pad + ROWS], precision="highest")
    stack = jnp.stack([kernel[r : r + NEAR] for r in range(ROWS)])
    hit = jnp.stack([src[r : r + NEAR] == own[r] for r in range(ROWS)])
    push = jnp.sum(jnp.where(hit[:, :, :, None, None], stack, 0.0), axis=2)
    return banded(pull.astype(BF16)), banded(jnp.flip(push, 3).astype(BF16))


def sum_kernel(axes, sizes, total, part, result, *scratch):
    slots = scratch[: len(axes)]
    send_sem, recv_sem = scratch[len(axes) :]
    places = [lax.axis_index(axis) for axis in axes]
    barrier = pltpu.get_barrier_semaphore()
    greeted = 0
    for axis, size, place in zip(axes, sizes, places):
        for d in range(1, size):
            peer = lax.rem(place + d, size)
            pl.semaphore_signal(barrier, inc=1, device_id={axis: peer}, device_id_type=pl.DeviceIdType.MESH)
            greeted += 1
    pl.semaphore_wait(barrier, greeted)

    used = 0
    base, extent = 0, total
    bases = []

    def block(ref, start, count):
        return ref.at[pl.ds(pl.multiple_of(start, 8), count)]

    for level, (axis, size, place) in enumerate(zip(axes, sizes, places)):
        bases.append((base, extent))
        extent //= size
        copies = []
        for d in range(1, size):
            peer = lax.rem(place + d, size)
            copy = pltpu.make_async_remote_copy(
                src_ref=block(part, base + peer * extent, extent),
                dst_ref=slots[level].at[d - 1],
                send_sem=send_sem.at[used],
                recv_sem=recv_sem.at[used],
                device_id={axis: peer},
                device_id_type=pl.DeviceIdType.MESH,
            )
            copy.start()
            copies.append(copy)
            used += 1
        base = base + place * extent
        for copy in copies:
            copy.wait()
        mine = pl.ds(pl.multiple_of(base, 8), extent)
        value = part[mine, :]
        for d in range(1, size):
            value = value + slots[level][d - 1]
        part[mine, :] = value
    result[mine, :] = value
    for level in reversed(range(len(axes))):
        axis, size, place = axes[level], sizes[level], places[level]
        outer, whole = bases[level]
        extent = whole // size
        copies = []
        for d in range(1, size):
            peer = lax.rem(place + d, size)
            own = outer + place * extent
            copy = pltpu.make_async_remote_copy(
                src_ref=block(result, own, extent),
                dst_ref=block(result, own, extent),
                send_sem=send_sem.at[used],
                recv_sem=recv_sem.at[used],
                device_id={axis: peer},
                device_id_type=pl.DeviceIdType.MESH,
            )
            copy.start()
            copies.append(copy)
            used += 1
        for copy in copies:
            copy.wait()


def summed(parts, scale):
    axes = ("ens", "lon", "lat")
    sizes = [lax.axis_size(axis) for axis in axes]
    rows = sum(part.shape[0] for part in parts)
    chan = parts[0].shape[1]
    devices = sizes[0] * sizes[1] * sizes[2]
    total = -(-rows // (8 * devices)) * 8 * devices
    filler = jnp.zeros((total - rows, chan), F32)
    stacked = jnp.concatenate([part * scale for part in parts] + [filler], axis=0)
    slots, extent, count = [], total, 0
    for size in sizes:
        extent //= size
        slots.append(pltpu.VMEM((size - 1, extent, chan), F32))
        count += 2 * (size - 1)

    def kernel(part, result, held, *scratch):
        held[...] = part[...]
        sum_kernel(axes, sizes, total, held, result, *scratch)

    vmem = pl.BlockSpec(memory_space=pltpu.VMEM)
    return pl.pallas_call(
        kernel,
        out_shape=jax.ShapeDtypeStruct((total, chan), F32),
        in_specs=[vmem],
        out_specs=vmem,
        scratch_shapes=[pltpu.VMEM((total, chan), F32)]
        + slots
        + [pltpu.SemaphoreType.DMA((count,)), pltpu.SemaphoreType.DMA((count,))],
        compiler_params=pltpu.CompilerParams(
            collective_id=0, has_side_effects=True, vmem_limit_bytes=32 * 2**20
        ),
        cost_estimate=pl.CostEstimate(flops=0, bytes_accessed=20 * 2**20, transcendentals=0),
    )(stacked)


def shards(fields, cotangent, filter_one, filter_two, mix_one, mix_two, source_rows, band_width):
    activ = fields[0]
    cot = cotangent[0]
    cols = activ.shape[1]
    wide = 2 * WHALF
    width = -(-(cols + wide) // TILE) * TILE
    total_rows = ROWS * lax.axis_size("lat")
    total_cols = cols * lax.axis_size("lon")
    first_row = lax.axis_index("lat") * ROWS

    lon = lax.axis_size("lon")
    head = jnp.stack([activ[:, :wide], cot[:, :wide]])
    tail = jnp.stack([activ[:, cols - wide :], cot[:, cols - wide :]])
    left = lax.ppermute(tail, "lon", [(i, (i + 1) % lon) for i in range(lon)])
    right = lax.ppermute(head, "lon", [((i + 1) % lon, i) for i in range(lon)])

    def widened(index, block):
        tail = jnp.zeros((ROWS, width + MARGIN - cols - 2 * wide, block.shape[2]), BF16)
        return jnp.concatenate([left[index], block, right[index], tail], axis=1)

    fields_halo = exchanged(widened(0, activ))
    cot_wide = widened(1, cot)
    cot_halo = exchanged(cot_wide)

    pull_one, push_one = filter_tables(masked_filters(filter_one, band_width), source_rows, first_row)
    pull_two, push_two = filter_tables(masked_filters(filter_two, band_width), source_rows, first_row)

    hidden, slope = layer("gate", cols, fields_halo, pull_one, mix_one)
    hidden_halo = exchanged(hidden)
    (pre_grad,) = layer("scale", cols, cot_halo, push_two, mix_two, turn=True, slope=slope)
    pre_halo = exchanged(pre_grad)
    inner = (WHALF, WHALF + cols)
    (part_one,) = layer("none", cols, fields_halo, pull_one, grad=pre_grad, valid=inner)
    forward, part_two = layer("plain", cols, hidden_halo, pull_two, mix_two, grad=cot, valid=(0, cols))
    (adjoint,) = layer("plain", cols, pre_halo, push_one, mix_one, turn=True)

    factor = 1.0 / jnp.sqrt(jnp.float32(total_rows * total_cols * lax.axis_size("ens")))
    sums = summed([part_one, part_two], factor)
    length = part_one.shape[0]
    total_one, total_two = sums[:length], sums[length : 2 * length]
    return forward[None], adjoint[None], total_one, total_two


def solution(mesh):
    field = P(("groups", "ens"), "lat", "lon", None)
    return jax.shard_map(
        shards,
        mesh=mesh,
        in_specs=(field, field, P(), P(), P(), P(), P(), P()),
        out_specs=(field, field, P("groups", None), P("groups", None)),
        check_vma=False,
    )
```

```python
import functools

import jax
import jax.numpy as jnp
import numpy as np
from jax import lax
from jax.experimental import pallas as pl
from jax.experimental.pallas import tpu as pltpu
from jax.sharding import PartitionSpec as P

K = 9
G = 8
HALO_R = 2
WHALF = 4
WIN = 9
ROWS = 2
NEAR = 2 * HALO_R + 1
TILE = 32
SPAN = TILE + 16
HALF = 256
MARGIN = 16

F32 = jnp.float32
BF16 = jnp.bfloat16


def group_windows(block, cg):
    lane = lax.broadcasted_iota(jnp.int32, (cg, block.shape[1]), 1)
    low = [jnp.where((lane >= g * cg) & (lane < (g + 1) * cg), block, 0.0) for g in range(G)]
    wide = jnp.concatenate(low[: G // 2], axis=0)[:, :HALF]
    rest = jnp.concatenate(low[G // 2 :], axis=0)[:, 128:]
    gap = jnp.zeros((HALF - wide.shape[0], HALF), F32)
    return jnp.concatenate([wide, gap], axis=0), jnp.concatenate([gap, rest], axis=0)


def layer_kernel(mode, width, cols, turn, valid, with_mix, with_grad, sharing, *refs):
    refs = list(refs)
    if sharing:
        refs, shared = refs[: -sharing[-1]], refs[-sharing[-1] :]
    up, own, down, band = refs[:4]
    refs = refs[4:]
    if with_mix:
        mix_ref = refs.pop(0)
    if mode == "scale":
        slope_in = refs.pop(0)
    if with_grad:
        grad_in = refs.pop(0)
        turned = refs.pop()
        padded = refs.pop()
    phases = iter(())
    if sharing:
        parts = [refs.pop(0), refs.pop(0)]
        phases = sum_phases(*sharing[:-1], parts, refs.pop(1), *shared)
    if with_mix:
        weights = refs[-2:]
        refs = refs[:-2]
    lows, highs = refs[-2:]
    refs = refs[:-2]
    rows = [up.at[0], up.at[1], own.at[0], own.at[1], down.at[0], down.at[1]]

    next(phases, None)
    if with_mix:
        cg = mix_ref.shape[1] // G

        def spread(k, carry):
            block = mix_ref[pl.ds(pl.multiple_of(k * cg, 16), cg), :].astype(F32)
            at = pl.ds(pl.multiple_of(k * HALF, HALF), HALF)
            for dest, window in zip(weights, group_windows(block, cg)):
                dest[at, :] = (window.T if turn else window).astype(BF16)
            return carry

        lax.fori_loop(0, K, spread, 0)

    def basis(b, carry):
        start = pl.multiple_of(b * TILE, TILE)
        for r in range(ROWS):
            slab = jnp.concatenate(
                [rows[r + e][pl.ds(start, SPAN), :] for e in range(NEAR)], axis=0
            )
            out = jnp.dot(band[r], slab, preferred_element_type=F32).astype(BF16)
            at = pl.multiple_of(r * width + start, TILE)
            for k in range(K):
                piece = out[k * TILE : (k + 1) * TILE]
                lows[pl.ds(at, TILE), k * HALF : (k + 1) * HALF] = piece[:, :HALF]
                highs[pl.ds(at, TILE), k * HALF : (k + 1) * HALF] = piece[:, 128:]
        return carry

    blocks = width // TILE
    lax.fori_loop(0, blocks // 2, basis, 0)
    next(phases, None)
    lax.fori_loop(blocks // 2, blocks, basis, 0)
    next(phases, None)

    if with_mix:
        step = width // 2

        def mix(r, carry):
            for part in range(2):
                at = pl.multiple_of(r * width + part * step, 16)
                low = jnp.dot(lows[pl.ds(at, step), :], weights[0][...], preferred_element_type=F32)
                high = jnp.dot(highs[pl.ds(at, step), :], weights[1][...], preferred_element_type=F32)
                total = jnp.concatenate(
                    [low[:, :128], low[:, 128:] + high[:, :128], high[:, 128:]], axis=1
                )
                span = slice(part * step, (part + 1) * step)
                if mode == "gate":
                    gate = jax.nn.sigmoid(total)
                    refs[0][r, span, :] = (total * gate).astype(BF16)
                    refs[1][r, span, :] = gate * (1.0 + total * (1.0 - gate))
                elif mode == "scale":
                    refs[0][r, span, :] = (total * slope_in[r, span, :]).astype(BF16)
                else:
                    keep = min(step, cols - part * step)
                    refs[0][r, part * step : part * step + keep, :] = total[:keep].astype(BF16)
            if mode != "plain":
                refs[0][r, width : width + MARGIN, :] = jnp.zeros((MARGIN, total.shape[1]), BF16)
            return carry

        for r in range(ROWS):
            lax.fori_loop(r, r + 1, mix, 0)
            next(phases, None)
        for _ in phases:
            pass

    if with_grad:
        out = refs[-1]
        cg = out.shape[1] // G
        first, last = valid
        size = grad_in.shape[1]
        for r in range(ROWS):
            padded[...] = jnp.zeros(padded.shape, F32)
            here = min(size, width)
            value = grad_in[r, :here, :].astype(F32)
            place = lax.broadcasted_iota(jnp.int32, value.shape, 0)
            padded[:here, :] = jnp.where((place >= first) & (place < last), value, 0.0)
            turned[r] = padded[...].T.astype(BF16)

        def grad(k, carry):
            at = pl.multiple_of(k * HALF, HALF)
            low = jnp.zeros((HALF, HALF), F32)
            high = jnp.zeros((HALF, HALF), F32)
            for r in range(ROWS):
                span = slice(r * width, (r + 1) * width)
                low += jnp.dot(turned[r, 0:HALF, :width], lows[span, pl.ds(at, HALF)], preferred_element_type=F32)
                high += jnp.dot(turned[r, 128:, :width], highs[span, pl.ds(at, HALF)], preferred_element_type=F32)
            low, high = low.T, high.T
            lane = lax.broadcasted_iota(jnp.int32, (cg, HALF), 1)
            sums = []
            for block, base, groups in ((low, 0, range(4)), (high, 128, range(4, 8))):
                total = jnp.zeros((cg, HALF), F32)
                for g in groups:
                    first = g * cg - base
                    inside = (lane >= first) & (lane < first + cg)
                    total = total + jnp.where(inside, block[first : first + cg], 0.0)
                sums.append(total)
            low, high = sums
            out[pl.ds(pl.multiple_of(k * cg, 8), cg), :] = jnp.concatenate(
                [low[:, :128], low[:, 128:] + high[:, :128], high[:, 128:]], axis=1
            )
            return carry

        lax.fori_loop(0, K, grad, 0)


def layer(mode, cols, halo, band, weights=None, turn=False, slope=None, grad=None, valid=None, parts=None, scale=None):
    chan = halo[1].shape[2]
    width = halo[1].shape[1] - MARGIN
    with_mix, with_grad = weights is not None, grad is not None
    args = list(halo) + [band]
    outs = []
    if with_mix:
        args.append(weights)
        held = width + MARGIN if mode != "plain" else cols
        outs.append(jax.ShapeDtypeStruct((ROWS, held, chan), BF16))
    if mode == "gate":
        outs.append(jax.ShapeDtypeStruct((ROWS, width, chan), F32))
    if mode == "scale":
        args.append(slope)
    sharing, shared, extra = None, [], {}
    if parts is not None:
        args += parts
        sharing, shared, outs_more = sum_plan(parts, scale)
        outs.append(outs_more)
        extra = dict(collective_id=0, has_side_effects=True)
    depth = ROWS * width
    if with_grad:
        args.append(grad)
        outs.append(jax.ShapeDtypeStruct((K * chan // G, chan), F32))
    scratch = [pltpu.VMEM((depth, K * HALF), BF16)] * 2
    if with_mix:
        scratch += [pltpu.VMEM((K * HALF, HALF), BF16)] * 2
    if with_grad:
        long = -(-width // 128) * 128
        scratch += [pltpu.VMEM((long, chan), F32), pltpu.VMEM((ROWS, chan, long), BF16)]
    vmem = pl.BlockSpec(memory_space=pltpu.VMEM)
    flops = 2 * ROWS * width * K * HALF * 2 * HALF * (1 + with_mix + with_grad)
    return pl.pallas_call(
        functools.partial(layer_kernel, mode, width, cols, turn, valid, with_mix, with_grad, sharing),
        out_shape=tuple(outs),
        in_specs=[vmem] * len(args),
        out_specs=tuple([vmem] * len(outs)),
        scratch_shapes=scratch + shared,
        compiler_params=pltpu.CompilerParams(vmem_limit_bytes=48 * 2**20, **extra),
        cost_estimate=pl.CostEstimate(flops=flops, bytes_accessed=10 * 2**20, transcendentals=0),
    )(*args)


def exchanged(block):
    count = lax.axis_size("lat")
    up = lax.ppermute(block, "lat", [(i, i + 1) for i in range(count - 1)])
    down = lax.ppermute(block, "lat", [(i + 1, i) for i in range(count - 1)])
    return up, block, down


def masked_filters(filt, band_width):
    offsets = jnp.abs(jnp.arange(WIN, dtype=jnp.int32) - WHALF)
    keep = offsets[None, None, :] <= band_width[:, :, None]
    return filt * keep[:, :, None, :].astype(filt.dtype)


def banded(table):
    chosen = (
        jnp.arange(SPAN)[None, None, :] - jnp.arange(TILE)[None, :, None]
        == jnp.arange(WIN)[:, None, None]
    ).astype(BF16)
    out = jnp.einsum("rekw,wtv->rktev", table, chosen, preferred_element_type=F32)
    return out.astype(BF16).reshape(ROWS, K * TILE, NEAR * SPAN)


def filter_tables(kernel, source_rows, first_row):
    pad = HALO_R
    near = jnp.arange(NEAR)
    kernel = jnp.pad(kernel.astype(F32), ((pad, pad), (0, 0), (0, 0), (0, 0)))
    src = jnp.pad(source_rows, ((pad, pad), (0, 0)), constant_values=-1)
    kernel = lax.dynamic_slice_in_dim(kernel, first_row, ROWS + 2 * pad, 0)
    src = lax.dynamic_slice_in_dim(src, first_row, ROWS + 2 * pad, 0)
    own = first_row + jnp.arange(ROWS)
    hit = src[pad : pad + ROWS, :, None] == own[:, None, None] - pad + near
    pull = jnp.einsum("rse,rskw->rekw", hit.astype(F32), kernel[pad : pad + ROWS], precision="highest")
    stack = jnp.stack([kernel[r : r + NEAR] for r in range(ROWS)])
    hit = jnp.stack([src[r : r + NEAR] == own[r] for r in range(ROWS)])
    push = jnp.sum(jnp.where(hit[:, :, :, None, None], stack, 0.0), axis=2)
    return banded(pull.astype(BF16)), banded(jnp.flip(push, 3).astype(BF16))


def sum_plan(parts, scale):
    axes = ("ens", "lon", "lat")
    sizes = [lax.axis_size(axis) for axis in axes]
    rows = sum(part.shape[0] for part in parts)
    chan = parts[0].shape[1]
    devices = sizes[0] * sizes[1] * sizes[2]
    total = -(-rows // (16 * devices)) * 16 * devices
    slots, extent, count = [], total, 0
    for size in sizes:
        extent //= size
        slots.append(pltpu.VMEM((size - 1, extent, chan), BF16))
        count += 2 * (size - 1)
    scratch = [pltpu.VMEM((total, chan), F32), pltpu.VMEM((total, chan), BF16)] + slots
    scratch += [pltpu.SemaphoreType.DMA((count,)), pltpu.SemaphoreType.DMA((count,))]
    return (axes, sizes, total, scale, len(scratch)), scratch, jax.ShapeDtypeStruct((total, chan), BF16)


def sum_phases(axes, sizes, total, scale, parts, result, held, wire, *scratch):
    slots = scratch[: len(axes)]
    send_sem, recv_sem = scratch[len(axes) :]
    places = [lax.axis_index(axis) for axis in axes]
    barrier = pltpu.get_barrier_semaphore()
    greeted = 0
    for axis, size, place in zip(axes, sizes, places):
        for d in range(1, size):
            peer = lax.rem(place + d, size)
            pl.semaphore_signal(barrier, inc=1, device_id={axis: peer}, device_id_type=pl.DeviceIdType.MESH)
            greeted += 1
    at = 0
    for part in parts:
        held[at : at + part.shape[0], :] = part[...] * scale
        at += part.shape[0]
    held[at:, :] = jnp.zeros((total - at, held.shape[1]), F32)
    wire[...] = held[...].astype(BF16)
    pl.semaphore_wait(barrier, greeted)

    used = 0
    base, extent = 0, total
    bases = []

    def block(ref, start, count):
        return ref.at[pl.ds(pl.multiple_of(start, 16), count)]

    for level, (axis, size, place) in enumerate(zip(axes, sizes, places)):
        bases.append((base, extent))
        extent //= size
        copies = []
        for d in range(1, size):
            peer = lax.rem(place + d, size)
            copy = pltpu.make_async_remote_copy(
                src_ref=block(wire, base + peer * extent, extent),
                dst_ref=slots[level].at[d - 1],
                send_sem=send_sem.at[used],
                recv_sem=recv_sem.at[used],
                device_id={axis: peer},
                device_id_type=pl.DeviceIdType.MESH,
            )
            copy.start()
            copies.append(copy)
            used += 1
        base = base + place * extent
        yield
        for copy in copies:
            copy.wait()
        mine = pl.ds(pl.multiple_of(base, 16), extent)
        value = held[mine, :]
        for d in range(1, size):
            value = value + slots[level][d - 1].astype(F32)
        if level < len(axes) - 1:
            held[mine, :] = value
            wire[mine, :] = value.astype(BF16)
    result[mine, :] = value.astype(BF16)
    for level in reversed(range(len(axes))):
        axis, size, place = axes[level], sizes[level], places[level]
        outer, whole = bases[level]
        extent = whole // size
        own = outer + place * extent
        copies = []
        for d in range(1, size):
            peer = lax.rem(place + d, size)
            copy = pltpu.make_async_remote_copy(
                src_ref=block(result, own, extent),
                dst_ref=block(result, own, extent),
                send_sem=send_sem.at[used],
                recv_sem=recv_sem.at[used],
                device_id={axis: peer},
                device_id_type=pl.DeviceIdType.MESH,
            )
            copy.start()
            copies.append(copy)
            used += 1
        yield
        for copy in copies:
            copy.wait()


def shards(fields, cotangent, filter_one, filter_two, mix_one, mix_two, source_rows, band_width):
    activ = fields[0]
    cot = cotangent[0]
    cols = activ.shape[1]
    wide = 2 * WHALF
    width = -(-(cols + wide) // TILE) * TILE
    total_rows = ROWS * lax.axis_size("lat")
    total_cols = cols * lax.axis_size("lon")
    first_row = lax.axis_index("lat") * ROWS

    lon = lax.axis_size("lon")
    head = jnp.stack([activ[:, :wide], cot[:, :wide]])
    tail = jnp.stack([activ[:, cols - wide :], cot[:, cols - wide :]])
    left = lax.ppermute(tail, "lon", [(i, (i + 1) % lon) for i in range(lon)])
    right = lax.ppermute(head, "lon", [((i + 1) % lon, i) for i in range(lon)])

    def widened(index, block):
        tail = jnp.zeros((ROWS, width + MARGIN - cols - 2 * wide, block.shape[2]), BF16)
        return jnp.concatenate([left[index], block, right[index], tail], axis=1)

    fields_halo = exchanged(widened(0, activ))
    cot_wide = widened(1, cot)
    cot_halo = exchanged(cot_wide)

    pull_one, push_one = filter_tables(masked_filters(filter_one, band_width), source_rows, first_row)
    pull_two, push_two = filter_tables(masked_filters(filter_two, band_width), source_rows, first_row)

    hidden, slope = layer("gate", cols, fields_halo, pull_one, mix_one)
    hidden_halo = exchanged(hidden)
    (pre_grad,) = layer("scale", cols, cot_halo, push_two, mix_two, turn=True, slope=slope)
    pre_halo = exchanged(pre_grad)
    inner = (WHALF, WHALF + cols)
    (part_one,) = layer("none", cols, fields_halo, pull_one, grad=pre_grad, valid=inner)
    forward, part_two = layer("plain", cols, hidden_halo, pull_two, mix_two, grad=cot, valid=(0, cols))
    factor = float(1.0 / np.sqrt(np.float32(total_rows * total_cols * lax.axis_size("ens"))))
    adjoint, sums = layer(
        "plain", cols, pre_halo, push_one, mix_one, turn=True, parts=[part_one, part_two], scale=factor
    )
    sums = sums.astype(F32)
    length = part_one.shape[0]
    total_one, total_two = sums[:length], sums[length : 2 * length]
    return forward[None], adjoint[None], total_one, total_two


def solution(mesh):
    field = P(("groups", "ens"), "lat", "lon", None)
    return jax.shard_map(
        shards,
        mesh=mesh,
        in_specs=(field, field, P(), P(), P(), P(), P(), P()),
        out_specs=(field, field, P("groups", None), P("groups", None)),
        check_vma=False,
    )
```

```python
import functools

import jax
import jax.numpy as jnp
import numpy as np
from jax import lax
from jax.experimental import pallas as pl
from jax.experimental.pallas import tpu as pltpu
from jax.sharding import PartitionSpec as P

K = 9
G = 8
HALO_R = 2
WHALF = 4
WIN = 9
ROWS = 2
NEAR = 2 * HALO_R + 1
TILE = 32
SPAN = TILE + 16
HALF = 256
MARGIN = 16

F32 = jnp.float32
BF16 = jnp.bfloat16


def group_windows(block, cg):
    lane = lax.broadcasted_iota(jnp.int32, (cg, block.shape[1]), 1)
    low = [jnp.where((lane >= g * cg) & (lane < (g + 1) * cg), block, 0.0) for g in range(G)]
    wide = jnp.concatenate(low[: G // 2], axis=0)[:, :HALF]
    rest = jnp.concatenate(low[G // 2 :], axis=0)[:, 128:]
    gap = jnp.zeros((HALF - wide.shape[0], HALF), F32)
    return jnp.concatenate([wide, gap], axis=0), jnp.concatenate([gap, rest], axis=0)


def layer_kernel(mode, width, cols, turn, valid, with_mix, with_grad, sharing, *refs):
    refs = list(refs)
    if sharing:
        refs, shared = refs[: -sharing[-1]], refs[-sharing[-1] :]
    up, own, down, band = refs[:4]
    refs = refs[4:]
    if with_mix:
        mix_ref = refs.pop(0)
    if mode == "scale":
        slope_in = refs.pop(0)
    if sharing:
        parts = [refs.pop(0) for _ in range(sharing[-2])]
    if with_grad:
        grad_in = refs.pop(0)
        turned = refs.pop()
        padded = refs.pop()
    phases = iter(())
    if sharing:
        phases = sum_phases(*sharing[:-2], parts, refs.pop(1), *shared)
    if with_mix:
        weights = refs[-2:]
        refs = refs[:-2]
    lows, highs = refs[-2:]
    refs = refs[:-2]
    rows = [up.at[0], up.at[1], own.at[0], own.at[1], down.at[0], down.at[1]]

    next(phases, None)
    if with_mix:
        cg = mix_ref.shape[1] // G

        def spread(k, carry):
            block = mix_ref[pl.ds(pl.multiple_of(k * cg, 16), cg), :].astype(F32)
            at = pl.ds(pl.multiple_of(k * HALF, HALF), HALF)
            for dest, window in zip(weights, group_windows(block, cg)):
                dest[at, :] = (window.T if turn else window).astype(BF16)
            return carry

        lax.fori_loop(0, K, spread, 0)

    def basis(b, carry):
        start = pl.multiple_of(b * TILE, TILE)
        for r in range(ROWS):
            slab = jnp.concatenate(
                [rows[r + e][pl.ds(start, SPAN), :] for e in range(NEAR)], axis=0
            )
            out = jnp.dot(band[r], slab, preferred_element_type=F32).astype(BF16)
            at = pl.multiple_of(r * width + start, TILE)
            for k in range(K):
                piece = out[k * TILE : (k + 1) * TILE]
                lows[pl.ds(at, TILE), k * HALF : (k + 1) * HALF] = piece[:, :HALF]
                highs[pl.ds(at, TILE), k * HALF : (k + 1) * HALF] = piece[:, 128:]
        return carry

    blocks = width // TILE
    lax.fori_loop(0, blocks // 2, basis, 0)
    next(phases, None)
    lax.fori_loop(blocks // 2, blocks, basis, 0)
    next(phases, None)

    if with_mix:
        step = width // 2

        def mix(r, carry):
            for part in range(2):
                at = pl.multiple_of(r * width + part * step, 16)
                low = jnp.dot(lows[pl.ds(at, step), :], weights[0][...], preferred_element_type=F32)
                high = jnp.dot(highs[pl.ds(at, step), :], weights[1][...], preferred_element_type=F32)
                total = jnp.concatenate(
                    [low[:, :128], low[:, 128:] + high[:, :128], high[:, 128:]], axis=1
                )
                span = slice(part * step, (part + 1) * step)
                if mode == "gate":
                    gate = jax.nn.sigmoid(total)
                    refs[0][r, span, :] = (total * gate).astype(BF16)
                    refs[1][r, span, :] = gate * (1.0 + total * (1.0 - gate))
                elif mode == "scale":
                    refs[0][r, span, :] = (total * slope_in[r, span, :]).astype(BF16)
                else:
                    keep = min(step, cols - part * step)
                    refs[0][r, part * step : part * step + keep, :] = total[:keep].astype(BF16)
            if mode != "plain":
                refs[0][r, width : width + MARGIN, :] = jnp.zeros((MARGIN, total.shape[1]), BF16)
            return carry

        for r in range(ROWS):
            lax.fori_loop(r, r + 1, mix, 0)
            next(phases, None)

    if with_grad:
        out = refs[-1]
        cg = out.shape[1] // G
        first, last = valid
        size = grad_in.shape[1]
        for r in range(ROWS):
            padded[...] = jnp.zeros(padded.shape, F32)
            here = min(size, width)
            value = grad_in[r, :here, :].astype(F32)
            place = lax.broadcasted_iota(jnp.int32, value.shape, 0)
            padded[:here, :] = jnp.where((place >= first) & (place < last), value, 0.0)
            turned[r] = padded[...].T.astype(BF16)

        def grad(k, carry):
            at = pl.multiple_of(k * HALF, HALF)
            low = jnp.zeros((HALF, HALF), F32)
            high = jnp.zeros((HALF, HALF), F32)
            for r in range(ROWS):
                span = slice(r * width, (r + 1) * width)
                low += jnp.dot(turned[r, 0:HALF, :width], lows[span, pl.ds(at, HALF)], preferred_element_type=F32)
                high += jnp.dot(turned[r, 128:, :width], highs[span, pl.ds(at, HALF)], preferred_element_type=F32)
            low, high = low.T, high.T
            lane = lax.broadcasted_iota(jnp.int32, (cg, HALF), 1)
            sums = []
            for block, base, groups in ((low, 0, range(4)), (high, 128, range(4, 8))):
                total = jnp.zeros((cg, HALF), F32)
                for g in groups:
                    first = g * cg - base
                    inside = (lane >= first) & (lane < first + cg)
                    total = total + jnp.where(inside, block[first : first + cg], 0.0)
                sums.append(total)
            low, high = sums
            out[pl.ds(pl.multiple_of(k * cg, 8), cg), :] = jnp.concatenate(
                [low[:, :128], low[:, 128:] + high[:, :128], high[:, 128:]], axis=1
            )
            return carry

        lax.fori_loop(0, K, grad, 0)

    for _ in phases:
        pass


def layer(mode, cols, halo, band, weights=None, turn=False, slope=None, grad=None, valid=None, parts=None, scale=None, ident=0):
    chan = halo[1].shape[2]
    width = halo[1].shape[1] - MARGIN
    with_mix, with_grad = weights is not None, grad is not None
    args = list(halo) + [band]
    outs = []
    if with_mix:
        args.append(weights)
        held = width + MARGIN if mode != "plain" else cols
        outs.append(jax.ShapeDtypeStruct((ROWS, held, chan), BF16))
    if mode == "gate":
        outs.append(jax.ShapeDtypeStruct((ROWS, width, chan), F32))
    if mode == "scale":
        args.append(slope)
    sharing, shared, extra = None, [], {}
    if parts is not None:
        args += parts
        sharing, shared, outs_more = sum_plan(parts, scale)
        outs.append(outs_more)
        extra = dict(collective_id=ident, has_side_effects=True)
    depth = ROWS * width
    if with_grad:
        args.append(grad)
        outs.append(jax.ShapeDtypeStruct((K * chan // G, chan), F32))
    scratch = [pltpu.VMEM((depth, K * HALF), BF16)] * 2
    if with_mix:
        scratch += [pltpu.VMEM((K * HALF, HALF), BF16)] * 2
    if with_grad:
        long = -(-width // 128) * 128
        scratch += [pltpu.VMEM((long, chan), F32), pltpu.VMEM((ROWS, chan, long), BF16)]
    vmem = pl.BlockSpec(memory_space=pltpu.VMEM)
    flops = 2 * ROWS * width * K * HALF * 2 * HALF * (1 + with_mix + with_grad)
    return pl.pallas_call(
        functools.partial(layer_kernel, mode, width, cols, turn, valid, with_mix, with_grad, sharing),
        out_shape=tuple(outs),
        in_specs=[vmem] * len(args),
        out_specs=tuple([vmem] * len(outs)),
        scratch_shapes=scratch + shared,
        compiler_params=pltpu.CompilerParams(vmem_limit_bytes=48 * 2**20, **extra),
        cost_estimate=pl.CostEstimate(flops=flops, bytes_accessed=10 * 2**20, transcendentals=0),
    )(*args)


def exchanged(block):
    count = lax.axis_size("lat")
    up = lax.ppermute(block, "lat", [(i, i + 1) for i in range(count - 1)])
    down = lax.ppermute(block, "lat", [(i + 1, i) for i in range(count - 1)])
    return up, block, down


def masked_filters(filt, band_width):
    offsets = jnp.abs(jnp.arange(WIN, dtype=jnp.int32) - WHALF)
    keep = offsets[None, None, :] <= band_width[:, :, None]
    return filt * keep[:, :, None, :].astype(filt.dtype)


def banded(table):
    chosen = (
        jnp.arange(SPAN)[None, None, :] - jnp.arange(TILE)[None, :, None]
        == jnp.arange(WIN)[:, None, None]
    ).astype(BF16)
    out = jnp.einsum("rekw,wtv->rktev", table, chosen, preferred_element_type=F32)
    return out.astype(BF16).reshape(ROWS, K * TILE, NEAR * SPAN)


def filter_tables(kernel, source_rows, first_row):
    pad = HALO_R
    near = jnp.arange(NEAR)
    kernel = jnp.pad(kernel.astype(F32), ((pad, pad), (0, 0), (0, 0), (0, 0)))
    src = jnp.pad(source_rows, ((pad, pad), (0, 0)), constant_values=-1)
    kernel = lax.dynamic_slice_in_dim(kernel, first_row, ROWS + 2 * pad, 0)
    src = lax.dynamic_slice_in_dim(src, first_row, ROWS + 2 * pad, 0)
    own = first_row + jnp.arange(ROWS)
    hit = src[pad : pad + ROWS, :, None] == own[:, None, None] - pad + near
    pull = jnp.einsum("rse,rskw->rekw", hit.astype(F32), kernel[pad : pad + ROWS], precision="highest")
    stack = jnp.stack([kernel[r : r + NEAR] for r in range(ROWS)])
    hit = jnp.stack([src[r : r + NEAR] == own[r] for r in range(ROWS)])
    push = jnp.sum(jnp.where(hit[:, :, :, None, None], stack, 0.0), axis=2)
    return banded(pull.astype(BF16)), banded(jnp.flip(push, 3).astype(BF16))


def sum_plan(parts, scale):
    axes = ("ens", "lon", "lat")
    sizes = [lax.axis_size(axis) for axis in axes]
    rows = sum(part.shape[0] for part in parts)
    chan = parts[0].shape[1]
    devices = sizes[0] * sizes[1] * sizes[2]
    total = -(-rows // (16 * devices)) * 16 * devices
    slots, extent, count = [], total, 0
    for size in sizes:
        extent //= size
        slots.append(pltpu.VMEM((size - 1, extent, chan), BF16))
        count += 2 * (size - 1)
    scratch = [pltpu.VMEM((total, chan), F32), pltpu.VMEM((total, chan), BF16)] + slots
    scratch += [pltpu.SemaphoreType.DMA((count,)), pltpu.SemaphoreType.DMA((count,))]
    return (axes, sizes, total, scale, len(parts), len(scratch)), scratch, jax.ShapeDtypeStruct((total, chan), BF16)


def sum_phases(axes, sizes, total, scale, parts, result, held, wire, *scratch):
    slots = scratch[: len(axes)]
    send_sem, recv_sem = scratch[len(axes) :]
    places = [lax.axis_index(axis) for axis in axes]
    barrier = pltpu.get_barrier_semaphore()
    greeted = 0
    for axis, size, place in zip(axes, sizes, places):
        for d in range(1, size):
            peer = lax.rem(place + d, size)
            pl.semaphore_signal(barrier, inc=1, device_id={axis: peer}, device_id_type=pl.DeviceIdType.MESH)
            greeted += 1
    at = 0
    for part in parts:
        held[at : at + part.shape[0], :] = part[...] * scale
        at += part.shape[0]
    held[at:, :] = jnp.zeros((total - at, held.shape[1]), F32)
    wire[...] = held[...].astype(BF16)
    pl.semaphore_wait(barrier, greeted)

    used = 0
    base, extent = 0, total
    bases = []

    def block(ref, start, count):
        return ref.at[pl.ds(pl.multiple_of(start, 16), count)]

    for level, (axis, size, place) in enumerate(zip(axes, sizes, places)):
        bases.append((base, extent))
        extent //= size
        copies = []
        for d in range(1, size):
            peer = lax.rem(place + d, size)
            copy = pltpu.make_async_remote_copy(
                src_ref=block(wire, base + peer * extent, extent),
                dst_ref=slots[level].at[d - 1],
                send_sem=send_sem.at[used],
                recv_sem=recv_sem.at[used],
                device_id={axis: peer},
                device_id_type=pl.DeviceIdType.MESH,
            )
            copy.start()
            copies.append(copy)
            used += 1
        base = base + place * extent
        yield
        for copy in copies:
            copy.wait()
        mine = pl.ds(pl.multiple_of(base, 16), extent)
        value = held[mine, :]
        for d in range(1, size):
            value = value + slots[level][d - 1].astype(F32)
        if level < len(axes) - 1:
            held[mine, :] = value
            wire[mine, :] = value.astype(BF16)
    result[mine, :] = value.astype(BF16)
    for level in reversed(range(len(axes))):
        axis, size, place = axes[level], sizes[level], places[level]
        outer, whole = bases[level]
        extent = whole // size
        own = outer + place * extent
        copies = []
        for d in range(1, size):
            peer = lax.rem(place + d, size)
            copy = pltpu.make_async_remote_copy(
                src_ref=block(result, own, extent),
                dst_ref=block(result, own, extent),
                send_sem=send_sem.at[used],
                recv_sem=recv_sem.at[used],
                device_id={axis: peer},
                device_id_type=pl.DeviceIdType.MESH,
            )
            copy.start()
            copies.append(copy)
            used += 1
        yield
        for copy in copies:
            copy.wait()


def shards(fields, cotangent, filter_one, filter_two, mix_one, mix_two, source_rows, band_width):
    activ = fields[0]
    cot = cotangent[0]
    cols = activ.shape[1]
    wide = 2 * WHALF
    width = -(-(cols + wide) // TILE) * TILE
    total_rows = ROWS * lax.axis_size("lat")
    total_cols = cols * lax.axis_size("lon")
    first_row = lax.axis_index("lat") * ROWS

    lon = lax.axis_size("lon")
    head = jnp.stack([activ[:, :wide], cot[:, :wide]])
    tail = jnp.stack([activ[:, cols - wide :], cot[:, cols - wide :]])
    left = lax.ppermute(tail, "lon", [(i, (i + 1) % lon) for i in range(lon)])
    right = lax.ppermute(head, "lon", [((i + 1) % lon, i) for i in range(lon)])

    rims = exchanged(jnp.concatenate([left, right], axis=2))
    tail = jnp.zeros((ROWS, width + MARGIN - cols - 2 * wide, activ.shape[2]), BF16)

    def widened(index, blocks):
        return tuple(
            jnp.concatenate([rim[index, :, :wide], block, rim[index, :, wide:], tail], axis=1)
            for rim, block in zip(rims, blocks)
        )

    fields_own = exchanged(activ)
    later, fields_own, rims = lax.optimization_barrier((cot, fields_own, rims))
    fields_halo = widened(0, fields_own)
    cot_parts = exchanged(later)

    pull_one, push_one = filter_tables(masked_filters(filter_one, band_width), source_rows, first_row)
    pull_two, push_two = filter_tables(masked_filters(filter_two, band_width), source_rows, first_row)

    hidden, slope = layer("gate", cols, fields_halo, pull_one, mix_one)
    hidden_halo = exchanged(hidden)
    cot_parts, rims, slope = lax.optimization_barrier((cot_parts, rims, slope))
    cot_halo = widened(1, cot_parts)
    (pre_grad,) = layer("scale", cols, cot_halo, push_two, mix_two, turn=True, slope=slope)
    pre_halo = exchanged(pre_grad)
    inner = (WHALF, WHALF + cols)
    factor = float(1.0 / np.sqrt(np.float32(total_rows * total_cols * lax.axis_size("ens"))))
    (part_one,) = layer("none", cols, fields_halo, pull_one, grad=pre_grad, valid=inner)
    forward, sum_one, part_two = layer(
        "plain", cols, hidden_halo, pull_two, mix_two, grad=cot, valid=(0, cols), parts=[part_one], scale=factor
    )
    adjoint, sum_two = layer(
        "plain", cols, pre_halo, push_one, mix_one, turn=True, parts=[part_two], scale=factor, ident=1
    )
    total_one = sum_one[: part_one.shape[0]].astype(F32)
    total_two = sum_two[: part_two.shape[0]].astype(F32)
    return forward[None], adjoint[None], total_one, total_two


def solution(mesh):
    field = P(("groups", "ens"), "lat", "lon", None)
    return jax.shard_map(
        shards,
        mesh=mesh,
        in_specs=(field, field, P(), P(), P(), P(), P(), P()),
        out_specs=(field, field, P("groups", None), P("groups", None)),
        check_vma=False,
    )
```
